32 devices in a mesh: ka: 8 (over z, core), kp: 4 (over y, x).
Axes of the slice: x: 2, y: 2, z: 4, core: 2. Of those that a mesh axis runs over, the one named last changes fastest.
Arguments:
- cond_pairs: bfloat16 [128, 512, 16], P(('ka', 'kp')), may hold values from -0.5 to 0.5
- val_pairs: bfloat16 [128, 512, 16], P('kp'), may hold values from -0.5 to 0.5
- w_store: bfloat16 [64, 512, 512], P('ka')
- q_table: int32 [128, 64], P(('ka', 'kp')), may hold values from 0 to 255, as said below
- q_to_irr: int32 [256], replicated, may hold values from 0 to 63, as said below
- g_perm: int32 [256, 512], replicated, may hold values from 0 to 511, each once within a row
- home_slot: int32 [64], replicated, may hold values from 0 to 63, as said below
Outputs:
- kernel_window: float32 [2048, 1024], P(('ka', 'kp'))
The draws below stay inside these ranges and needn't reach their ends.
Inputs may be any that keep to these rules, and one draw needn't show every extreme that they name: `q_to_irr`: each irreducible index is named by exactly 4 momentum transfers. `home_slot`: A permutation of the storage positions. `g_perm`: each row is a permutation of the plane waves. `q_table`: for the 4 rows of one device and either half of the columns, the transfers name at most one irreducible block whose storage position lies in each run of 8 positions, and at most 24 slots name the same irreducible block; the second bound is reached for every device and half.
All inputs are finite; a program needn't handle non-finite values.
Results may differ from the reference program's by a relative error of at most 0.003.
Values may be sent and summed in bfloat16 or wider, within the bound.
A program may use at most 128 MiB of HBM per device.

```python
import jax
import jax.numpy as jnp
from jax import lax

G = 512
P_SIZE = 16
NSYM = 4
IRR_DEV = 8
KR = 4
KP = 32
NKW = 128
PCAP = 24
NIRR = 64
NQ = 256
N_KP = 4


def shared_tables(key):
    transfer_order = jax.random.permutation(jax.random.fold_in(key, 101), NQ).astype(jnp.int32)
    store_order = jax.random.permutation(jax.random.fold_in(key, 102), NIRR).astype(jnp.int32)
    return (transfer_order, store_order)


def draw_q_to_irr(key, part):
    transfer_order, store_order = shared_tables(key)
    return (transfer_order // NSYM).astype(jnp.int32)


def draw_home_slot(key, part):
    transfer_order, store_order = shared_tables(key)
    return store_order


def draw_q_table(key, part):
    transfer_order, store_order = shared_tables(key)
    key = jax.random.fold_in(key, 3)
    transfer_at = jnp.argsort(transfer_order).astype(jnp.int32)
    irr_at = jnp.argsort(store_order).astype(jnp.int32)
    owners = KP // KR
    fewest = owners * 3 // 4
    pair_count = KR * KP

    def one_tile(tile_index):
        sub_keys = jax.random.split(jax.random.fold_in(key, tile_index), 5)
        used_count = jax.random.randint(sub_keys[0], (), fewest, owners + 1)
        owner_order = jax.random.permutation(sub_keys[1], owners).astype(jnp.int32)
        slot_draw = jax.random.randint(sub_keys[2], (owners,), 0, IRR_DEV)
        position = jax.random.permutation(sub_keys[3], pair_count).astype(jnp.int32)
        slot_rank = jnp.where(position < PCAP, 0, 1 + (position - PCAP) % (used_count - 1))
        owner_of = owner_order[slot_rank]
        irr_index = irr_at[owner_of * IRR_DEV + slot_draw[owner_of]]
        image_of = jax.random.randint(sub_keys[4], (pair_count,), 0, NSYM)
        return transfer_at[irr_index * NSYM + image_of].reshape(KR, KP)
    tiles = jax.vmap(one_tile)(jnp.arange(2 * (NKW // KR), dtype=jnp.int32))
    tiles = tiles.reshape(NKW // KR, 2, KR, KP).transpose(0, 2, 1, 3)
    return tiles.reshape(NKW, 2 * KP).astype(jnp.int32)


def draw_w_store(key, part):
    key = jax.random.fold_in(key, 11)
    sub_keys = jax.random.split(key, 2)
    diagonal = jnp.exp(jax.random.uniform(sub_keys[0], (NIRR, G), jnp.float32, 0.0, jnp.log(8.0)))
    spread_part = jax.random.normal(sub_keys[1], (NIRR, G, G), jnp.float32) * G ** (-0.5)
    identity = jnp.eye(G, dtype=jnp.float32)
    return (spread_part + identity[None, :, :] * diagonal[:, :, None]).astype(jnp.bfloat16)


def level_of(key, dims, cuts, low, high):
    gain, own = 1.0, jax.random.fold_in(key, 6)
    for axis_at, shards_of in cuts:
        draws = jnp.exp(jax.random.uniform(jax.random.fold_in(own, axis_at), (shards_of,), jnp.float32, low / len(cuts), high / len(cuts)))
        gain = gain * jnp.repeat(draws, dims[axis_at] // shards_of).reshape([-1 if axis == axis_at else 1 for axis in range(len(dims))])
    return gain


def bell_draw(key, extent, deviation, most, cuts=(), kind=jnp.bfloat16):
    drawn = jax.random.normal(key, extent, jnp.float32) * deviation
    if len(cuts) > 0:
        drawn = level_of(key, extent, cuts, -0.22, 0.18) * drawn
    return jnp.clip(drawn, min=-most, max=most).astype(kind)


def setup_inputs(seed: int = 0) -> dict:
    key_of = jax.random.split(jax.random.key(seed), 8)
    return {
        "cond_pairs": bell_draw(key_of[0], (NKW, G, P_SIZE), 0.09, 0.5, ((0, 32),)),
        "val_pairs": bell_draw(key_of[1], (NKW, G, P_SIZE), 0.09, 0.5, ((0, 4),)),
        "w_store": draw_w_store(jax.random.fold_in(key_of[7], 71), 0),
        "q_table": draw_q_table(jax.random.fold_in(key_of[7], 71), 0),
        "q_to_irr": draw_q_to_irr(jax.random.fold_in(key_of[7], 71), 0),
        "g_perm": jax.vmap(lambda own: jax.random.permutation(own, G))(jax.random.split(key_of[5], NQ)).reshape((NQ, G)).astype(jnp.int32),
        "home_slot": draw_home_slot(jax.random.fold_in(key_of[7], 71), 0),
    }


def reference(cond_pairs, val_pairs, w_store, q_table, q_to_irr, g_perm, home_slot):
    columns_all = jnp.arange(2 * KP, dtype=jnp.int32)
    stop_of = columns_all // KP
    within_panel = columns_all % KP

    def one_row(row_index):
        row_group = row_index // KR
        panel_of = (row_group % N_KP - stop_of) % N_KP
        columns = (panel_of * KP + within_panel).astype(jnp.int32)
        transfers = q_table[row_index]
        shuffle = g_perm[transfers]
        blocks = w_store[home_slot[q_to_irr[transfers]]].astype(jnp.float32)
        val_rows = val_pairs[columns[:, None], shuffle].astype(jnp.float32)
        cond_rows = cond_pairs[row_index][shuffle].astype(jnp.float32)
        carried = jnp.einsum("ngh,nhp->ngp", blocks, val_rows, precision=lax.Precision.HIGHEST).astype(jnp.bfloat16)
        carried = lax.optimization_barrier(carried).astype(jnp.float32)
        kernel_row_block = -jnp.einsum("ngi,ngj->nij", cond_rows, carried, precision=lax.Precision.HIGHEST)
        return kernel_row_block.transpose(1, 0, 2).reshape(P_SIZE, 2 * KP * P_SIZE)

    all_rows = lax.map(one_row, jnp.arange(NKW, dtype=jnp.int32))
    return all_rows.reshape(NKW * P_SIZE, 2 * KP * P_SIZE)
```

```python
import functools

import jax
import jax.numpy as jnp
from jax import lax
from jax.experimental import pallas as pl
from jax.experimental.pallas import tpu as pltpu
from jax.sharding import PartitionSpec as P

NSYM = 4
CHUNK = 8


def pair_lists(q_all, q_to_irr, home_slot, per_owner, capacity):
    me = lax.axis_index("ka")
    i32 = jnp.int32
    irr_ids = jnp.arange(home_slot.shape[0], dtype=i32)
    stored = jnp.sum(
        jnp.where(q_to_irr[:, None] == irr_ids[None, :], home_slot[None, :], 0), axis=1
    )
    member = (stored // per_owner) == me
    q_count = q_to_irr.shape[0]
    q_ids = jnp.arange(q_count, dtype=i32)
    local_q = per_owner * NSYM
    rank = jnp.sum((member[None, :] & (q_ids[None, :] < q_ids[:, None])).astype(i32), axis=1)
    t_ids = jnp.arange(local_q, dtype=i32)
    at_t = member[None, :] & (rank[None, :] == t_ids[:, None])
    q_of = jnp.sum(jnp.where(at_t, q_ids[None, :], 0), axis=1)
    block_of = jnp.sum(jnp.where(at_t, stored[None, :] % per_owner, 0), axis=1)

    pairs = q_all.reshape(-1)
    pair_count = pairs.shape[0]
    run = 128
    same = (pairs.reshape(1, -1, run) == q_of[:, None, None])
    before = (jnp.arange(run)[:, None] < jnp.arange(run)[None, :]).astype(jnp.bfloat16)
    within = lax.dot_general(
        same.astype(jnp.bfloat16).reshape(-1, run), before, (((1,), (0,)), ((), ())),
        preferred_element_type=jnp.float32,
    ).astype(i32).reshape(same.shape)
    per_run = jnp.sum(same.astype(i32), axis=2)
    runs = per_run.shape[1]
    run_ids = jnp.arange(runs, dtype=i32)
    run_start = jnp.sum(
        jnp.where(run_ids[None, :, None] > run_ids[None, None, :], per_run[:, None, :], 0), axis=2
    )
    count = jnp.sum(per_run, axis=1)
    chunks = (count + CHUNK - 1) // CHUNK
    first = jnp.sum(jnp.where(t_ids[:, None] > t_ids[None, :], chunks[None, :], 0), axis=1)
    place = (first * CHUNK)[:, None, None] + run_start[:, :, None] + within
    position = jnp.sum(jnp.where(same, place + 1, 0), axis=0).reshape(-1) - 1
    slots = capacity + local_q * CHUNK
    slot_ids = jnp.arange(slots, dtype=i32)
    pair_ids = jnp.arange(pair_count, dtype=i32)
    table = jnp.sum(
        jnp.where(position[None, :] == slot_ids[:, None], pair_ids[None, :] + 1, 0), axis=1
    ) - 1
    meta = jnp.stack([q_of, block_of, first, chunks])
    return table, meta


def owner_kernel(table, meta, val_ref, cond_ref, w_ref, perm_ref, out_ref, rows, shuffle):
    half = CHUNK * 16
    g = w_ref.shape[1]
    columns = val_ref.shape[0]
    local_q = meta.shape[1]
    out_ref[...] = jnp.zeros_like(out_ref)
    lane_group = lax.broadcasted_iota(jnp.int32, (16, 128), 1) // 16

    def one_transfer(t, carry):
        chunks = meta[3, t]

        @pl.when(chunks > 0)
        def _():
            order = perm_ref[pl.ds(meta[0, t], 1), :]
            g_ids = lax.broadcasted_iota(jnp.int32, (g, g), 0)
            shuffle[...] = jnp.where(g_ids == order, 1.0, 0.0).astype(jnp.bfloat16)
            block = meta[1, t]

            def one_chunk(step, inner):
                base = (meta[2, t] + step) * CHUNK
                for p in range(CHUNK):
                    pair = jnp.maximum(table[base + p], 0)
                    rows[p * 16:(p + 1) * 16, :] = val_ref[pair % columns]
                    rows[half + p * 16:half + (p + 1) * 16, :] = cond_ref[pair // columns]
                moved = jnp.dot(
                    rows[...], shuffle[...], preferred_element_type=jnp.float32
                ).astype(jnp.bfloat16)
                carried = lax.dot_general(
                    moved[:half], w_ref[block], (((1,), (1,)), ((), ())),
                    preferred_element_type=jnp.float32,
                ).astype(jnp.bfloat16)
                products = -lax.dot_general(
                    moved[half:], carried, (((1,), (1,)), ((), ())),
                    preferred_element_type=jnp.float32,
                )
                for p in range(CHUNK):
                    pair = table[base + p]

                    @pl.when(pair >= 0)
                    def _(p=p, pair=pair):
                        row, col = pair // columns, pair % columns
                        group = col % 8
                        turned = pltpu.roll(
                            products[p * 16:(p + 1) * 16, :], ((group - p + 8) % 8) * 16, 1
                        ).astype(jnp.bfloat16)
                        at = pl.ds(pl.multiple_of((col // 8) * 128, 128), 128)
                        out_ref[row, :, at] = jnp.where(
                            lane_group == group, turned, out_ref[row, :, at]
                        )
                return inner

            lax.fori_loop(0, chunks, one_chunk, 0)
        return carry

    lax.fori_loop(0, local_q, one_transfer, 0)


def owner_products(table, meta, val_t, cond_t, w_store, g_perm):
    rows, band_pairs, g = cond_t.shape
    columns = val_t.shape[0]
    vmem = pl.BlockSpec(memory_space=pltpu.VMEM)
    smem = pl.BlockSpec(memory_space=pltpu.SMEM)
    return pl.pallas_call(
        owner_kernel,
        out_shape=jax.ShapeDtypeStruct((rows, band_pairs, columns * band_pairs), jnp.bfloat16),
        in_specs=[smem, smem, vmem, vmem, vmem, vmem],
        out_specs=vmem,
        scratch_shapes=[
            pltpu.VMEM((2 * CHUNK * band_pairs, g), jnp.bfloat16),
            pltpu.VMEM((g, g), jnp.bfloat16),
        ],
        compiler_params=pltpu.CompilerParams(vmem_limit_bytes=48 * 1024 * 1024),
        cost_estimate=pl.CostEstimate(
            flops=10_000_000_000, bytes_accessed=8_000_000, transcendentals=0
        ),
    )(table, meta, val_t, cond_t, w_store, g_perm)


def per_device(cond_pairs, val_pairs, w_store, q_table, q_to_irr, g_perm, home_slot):
    owners = lax.axis_size("ka")
    peers = lax.axis_size("kp")
    per_owner = w_store.shape[0]
    row_count = cond_pairs.shape[0]
    band_pairs = cond_pairs.shape[2]
    q_all = lax.all_gather(q_table, "ka", axis=0, tiled=True)
    cond_t = lax.all_gather(cond_pairs.transpose(0, 2, 1), "ka", axis=0, tiled=True)
    own_t = val_pairs.transpose(0, 2, 1)
    next_t = lax.ppermute(own_t, "kp", [(i, (i + 1) % peers) for i in range(peers)])
    val_t = jnp.concatenate([own_t, next_t], axis=0)
    capacity = owners * 2 * (3 * row_count * row_count // 2)
    table, meta = pair_lists(q_all, q_to_irr, home_slot, per_owner, capacity)
    parts = owner_products(table, meta, val_t, cond_t, w_store, g_perm)
    columns = val_t.shape[0] * band_pairs
    parts = parts.reshape(owners, row_count * band_pairs, columns)
    back = lax.all_to_all(parts, "ka", split_axis=0, concat_axis=0, tiled=True)
    return jnp.sum(back.astype(jnp.float32), axis=0)


def solution(mesh):
    placed = (
        P(("ka", "kp"), None, None),
        P("kp", None, None),
        P("ka", None, None),
        P(("ka", "kp"), None),
        P(),
        P(),
        P(),
    )
    return jax.shard_map(
        per_device, mesh=mesh, in_specs=placed, out_specs=P(("ka", "kp"), None), check_vma=False
    )
```

```python
import functools

import jax
import jax.numpy as jnp
from jax import lax
from jax.experimental import pallas as pl
from jax.experimental.pallas import tpu as pltpu
from jax.sharding import PartitionSpec as P

NSYM = 4
CHUNK = 8
MESH = pl.DeviceIdType.MESH


def pair_lists(q_all, q_to_irr, home_slot, per_owner, capacity):
    me = lax.axis_index("ka")
    i32 = jnp.int32
    irr_ids = jnp.arange(home_slot.shape[0], dtype=i32)
    stored = jnp.sum(
        jnp.where(q_to_irr[:, None] == irr_ids[None, :], home_slot[None, :], 0), axis=1
    )
    member = (stored // per_owner) == me
    q_count = q_to_irr.shape[0]
    q_ids = jnp.arange(q_count, dtype=i32)
    local_q = per_owner * NSYM
    rank = jnp.sum((member[None, :] & (q_ids[None, :] < q_ids[:, None])).astype(i32), axis=1)
    t_ids = jnp.arange(local_q, dtype=i32)
    at_t = member[None, :] & (rank[None, :] == t_ids[:, None])
    q_of = jnp.sum(jnp.where(at_t, q_ids[None, :], 0), axis=1)
    block_of = jnp.sum(jnp.where(at_t, stored[None, :] % per_owner, 0), axis=1)

    pairs = q_all.reshape(-1)
    pair_count = pairs.shape[0]
    run = 128
    same = (pairs.reshape(1, -1, run) == q_of[:, None, None])
    before = (jnp.arange(run)[:, None] < jnp.arange(run)[None, :]).astype(jnp.bfloat16)
    within = lax.dot_general(
        same.astype(jnp.bfloat16).reshape(-1, run), before, (((1,), (0,)), ((), ())),
        preferred_element_type=jnp.float32,
    ).astype(i32).reshape(same.shape)
    per_run = jnp.sum(same.astype(i32), axis=2)
    runs = per_run.shape[1]
    run_ids = jnp.arange(runs, dtype=i32)
    run_start = jnp.sum(
        jnp.where(run_ids[None, :, None] > run_ids[None, None, :], per_run[:, None, :], 0), axis=2
    )
    count = jnp.sum(per_run, axis=1)
    chunks = (count + CHUNK - 1) // CHUNK
    first = jnp.sum(jnp.where(t_ids[:, None] > t_ids[None, :], chunks[None, :], 0), axis=1)
    place = (first * CHUNK)[:, None, None] + run_start[:, :, None] + within
    position = jnp.sum(jnp.where(same, place + 1, 0), axis=0).reshape(-1) - 1
    slots = capacity + local_q * CHUNK
    slot_ids = jnp.arange(slots, dtype=i32)
    pair_ids = jnp.arange(pair_count, dtype=i32)
    filled = jnp.sum(
        jnp.where(position[None, :] == slot_ids[:, None], pair_ids[None, :] + 1, 0), axis=1
    ).reshape(-1, CHUNK)
    table = jnp.where(filled > 0, filled, filled[:, :1]).reshape(-1) - 1
    table = jnp.maximum(table, 0)
    chunk_ids = jnp.arange(slots // CHUNK, dtype=i32)
    of_chunk = (first[:, None] <= chunk_ids[None, :]) & (
        chunk_ids[None, :] < (first + chunks)[:, None]
    )
    chunk_q = jnp.sum(jnp.where(of_chunk, q_of[:, None], 0), axis=0)
    chunk_block = jnp.sum(jnp.where(of_chunk, block_of[:, None], 0), axis=0)
    used = jnp.broadcast_to(jnp.sum(chunks), chunk_q.shape)
    return table, jnp.stack([chunk_q, chunk_block, used])


def owner_kernel(table, meta, val_ref, cond_ref, w_ref, perm_ref, out_ref,
                 rows_a, rows_b, moved_a, moved_b, shuffle_a, shuffle_b):
    half = CHUNK * 16
    g = w_ref.shape[1]
    columns = val_ref.shape[0]
    chunks = meta[2, 0]
    lane_group = lax.broadcasted_iota(jnp.int32, (16, 128), 1) // 16
    out_ref[...] = jnp.zeros_like(out_ref)

    def row_col(pair):
        if columns & (columns - 1) == 0:
            return pair >> (columns.bit_length() - 1), pair & (columns - 1)
        return pair // columns, pair % columns

    def permute(chunk, rows, moved, shuffle):
        chunk = jnp.minimum(chunk, chunks - 1)
        order = perm_ref[pl.ds(meta[0, chunk], 1), :]
        g_ids = lax.broadcasted_iota(jnp.int32, (g, g), 0)
        shuffle[...] = jnp.where(g_ids == order, 1.0, 0.0).astype(jnp.bfloat16)
        for p in range(CHUNK):
            row, col = row_col(table[chunk * CHUNK + p])
            rows[p * 16:(p + 1) * 16, :] = val_ref[col]
            rows[half + p * 16:half + (p + 1) * 16, :] = cond_ref[row]
        moved[...] = jnp.dot(
            rows[...], shuffle[...], preferred_element_type=jnp.float32
        ).astype(jnp.bfloat16)

    def multiply(chunk, moved):
        chunk = jnp.minimum(chunk, chunks - 1)
        carried = lax.dot_general(
            moved[:half, :], w_ref[meta[1, chunk]], (((1,), (1,)), ((), ())),
            preferred_element_type=jnp.float32,
        ).astype(jnp.bfloat16)
        products = -lax.dot_general(
            moved[half:, :], carried, (((1,), (1,)), ((), ())),
            preferred_element_type=jnp.float32,
        )
        for p in range(CHUNK):
            row, col = row_col(table[chunk * CHUNK + p])
            group = col & 7
            turned = pltpu.roll(
                products[p * 16:(p + 1) * 16, :], ((group - p + 8) & 7) * 16, 1
            ).astype(jnp.bfloat16)
            at = pl.ds(pl.multiple_of((col >> 3) * 128, 128), 128)
            out_ref[row, :, at] = jnp.where(lane_group == group, turned, out_ref[row, :, at])

    @pl.when(chunks > 0)
    def _():
        permute(0, rows_a, moved_a, shuffle_a)

        def two_chunks(i, carry):
            permute(2 * i + 1, rows_b, moved_b, shuffle_b)
            multiply(2 * i, moved_a)
            permute(2 * i + 2, rows_a, moved_a, shuffle_a)
            multiply(2 * i + 1, moved_b)
            return carry

        lax.fori_loop(0, (chunks + 1) // 2, two_chunks, 0)


def owner_products(table, meta, val_t, cond_t, w_store, g_perm):
    rows, band_pairs, g = cond_t.shape
    columns = val_t.shape[0]
    vmem = pl.BlockSpec(memory_space=pltpu.VMEM)
    smem = pl.BlockSpec(memory_space=pltpu.SMEM)
    return pl.pallas_call(
        owner_kernel,
        out_shape=jax.ShapeDtypeStruct((rows, band_pairs, columns * band_pairs), jnp.bfloat16),
        in_specs=[smem, smem, vmem, vmem, vmem, vmem],
        out_specs=vmem,
        scratch_shapes=[
            *[pltpu.VMEM((2 * CHUNK * band_pairs, g), jnp.bfloat16)] * 4,
            *[pltpu.VMEM((g, g), jnp.bfloat16)] * 2,
        ],
        compiler_params=pltpu.CompilerParams(vmem_limit_bytes=48 * 1024 * 1024),
        cost_estimate=pl.CostEstimate(
            flops=10_000_000_000, bytes_accessed=8_000_000, transcendentals=0
        ),
    )(table, meta, val_t, cond_t, w_store, g_perm)


def gather_kernel(owners, peers, q_ref, cond_ref, val_ref, q_out, cond_out, val_out,
                  q_send, q_recv, cond_send, cond_recv, val_send, val_recv, own_sem):
    a, p = lax.axis_index("ka"), lax.axis_index("kp")
    ahead, behind = lax.rem(p + 1, peers), lax.rem(p + peers - 1, peers)
    width = val_ref.shape[0]
    barrier = pltpu.get_barrier_semaphore()
    for step in range(1, owners):
        pl.semaphore_signal(
            barrier, inc=1, device_id=(lax.rem(a + step, owners), p), device_id_type=MESH
        )
    for other in (ahead, behind):
        pl.semaphore_signal(barrier, inc=1, device_id=(a, other), device_id_type=MESH)
    pl.semaphore_wait(barrier, owners + 1)
    copies = []
    for source, target, send, recv in (
        (q_ref, q_out, q_send, q_recv), (cond_ref, cond_out, cond_send, cond_recv)
    ):
        for step in range(1, owners):
            copy = pltpu.make_async_remote_copy(
                src_ref=source, dst_ref=target.at[a],
                send_sem=send.at[step - 1], recv_sem=recv.at[step - 1],
                device_id=(lax.rem(a + step, owners), p), device_id_type=MESH,
            )
            copy.start()
            copies.append(copy)
        if source is q_ref:
            copy = pltpu.make_async_remote_copy(
                src_ref=val_ref, dst_ref=val_out.at[pl.ds(width, width)],
                send_sem=val_send, recv_sem=val_recv,
                device_id=(a, ahead), device_id_type=MESH,
            )
            copy.start()
            copies.append(copy)
    own = [
        pltpu.make_async_copy(q_ref, q_out.at[a], own_sem.at[0]),
        pltpu.make_async_copy(cond_ref, cond_out.at[a], own_sem.at[1]),
        pltpu.make_async_copy(val_ref, val_out.at[pl.ds(0, width)], own_sem.at[2]),
    ]
    for copy in own:
        copy.start()
    for copy in own:
        copy.wait()
    for copy in copies:
        copy.wait()


def gathered(owners, peers, q_table, cond_t, val_t):
    anywhere = pl.BlockSpec(memory_space=pl.ANY)
    dma = pltpu.SemaphoreType.DMA
    return pl.pallas_call(
        functools.partial(gather_kernel, owners, peers),
        out_shape=(
            jax.ShapeDtypeStruct((owners, *q_table.shape), q_table.dtype),
            jax.ShapeDtypeStruct((owners, *cond_t.shape), cond_t.dtype),
            jax.ShapeDtypeStruct((2 * val_t.shape[0], *val_t.shape[1:]), val_t.dtype),
        ),
        in_specs=[anywhere] * 3,
        out_specs=(anywhere,) * 3,
        scratch_shapes=[
            dma((owners - 1,)), dma((owners - 1,)), dma((owners - 1,)), dma((owners - 1,)),
            dma, dma, dma((3,)),
        ],
        compiler_params=pltpu.CompilerParams(collective_id=0, has_side_effects=True),
    )(q_table, cond_t, val_t)


def return_kernel(owners, parts_ref, out_ref, landed, send, recv, own_sem):
    a, p = lax.axis_index("ka"), lax.axis_index("kp")
    barrier = pltpu.get_barrier_semaphore()
    for step in range(1, owners):
        pl.semaphore_signal(
            barrier, inc=1, device_id=(lax.rem(a + step, owners), p), device_id_type=MESH
        )
    pl.semaphore_wait(barrier, owners - 1)
    copies = []
    for step in range(1, owners):
        peer = lax.rem(a + step, owners)
        copy = pltpu.make_async_remote_copy(
            src_ref=parts_ref.at[peer], dst_ref=landed.at[step],
            send_sem=send.at[step - 1], recv_sem=recv.at[step - 1],
            device_id=(peer, p), device_id_type=MESH,
        )
        copy.start()
        copies.append(copy)
    own = pltpu.make_async_copy(parts_ref.at[a], landed.at[0], own_sem)
    own.start()
    own.wait()
    out_ref[...] = landed[0].astype(jnp.float32)
    for step in range(1, owners):
        copies[step - 1].wait()
        out_ref[...] += landed[step].astype(jnp.float32)


def returned(owners, parts):
    dma = pltpu.SemaphoreType.DMA
    return pl.pallas_call(
        functools.partial(return_kernel, owners),
        out_shape=jax.ShapeDtypeStruct(parts.shape[1:], jnp.float32),
        in_specs=[pl.BlockSpec(memory_space=pl.ANY)],
        out_specs=pl.BlockSpec(memory_space=pltpu.VMEM),
        scratch_shapes=[
            pltpu.VMEM(parts.shape, parts.dtype), dma((owners - 1,)), dma((owners - 1,)), dma,
        ],
        compiler_params=pltpu.CompilerParams(
            collective_id=1, has_side_effects=True, vmem_limit_bytes=32 * 1024 * 1024
        ),
    )(parts)


def per_device(cond_pairs, val_pairs, w_store, q_table, q_to_irr, g_perm, home_slot):
    owners = lax.axis_size("ka")
    peers = lax.axis_size("kp")
    per_owner = w_store.shape[0]
    row_count = cond_pairs.shape[0]
    band_pairs = cond_pairs.shape[2]
    q_all, cond_t, val_t = gathered(
        owners, peers, q_table, cond_pairs.transpose(0, 2, 1), val_pairs.transpose(0, 2, 1)
    )
    cond_t = cond_t.reshape(owners * row_count, band_pairs, -1)
    capacity = owners * 2 * (3 * row_count * row_count // 2)
    table, meta = pair_lists(q_all, q_to_irr, home_slot, per_owner, capacity)
    parts = owner_products(table, meta, val_t, cond_t, w_store, g_perm)
    columns = val_t.shape[0] * band_pairs
    parts = parts.reshape(owners, row_count * band_pairs, columns)
    return returned(owners, parts)


def solution(mesh):
    placed = (
        P(("ka", "kp"), None, None),
        P("kp", None, None),
        P("ka", None, None),
        P(("ka", "kp"), None),
        P(),
        P(),
        P(),
    )
    return jax.shard_map(
        per_device, mesh=mesh, in_specs=placed, out_specs=P(("ka", "kp"), None), check_vma=False
    )
```

```python
import functools

import jax
import jax.numpy as jnp
from jax import lax
from jax.experimental import pallas as pl
from jax.experimental.pallas import tpu as pltpu
from jax.sharding import PartitionSpec as P

NSYM = 4
CHUNK = 8
MESH = pl.DeviceIdType.MESH


def pair_lists(q_all, q_to_irr, home_slot, per_owner, capacity):
    me = lax.axis_index("ka")
    i32 = jnp.int32
    irr_ids = jnp.arange(home_slot.shape[0], dtype=i32)
    stored = jnp.sum(
        jnp.where(q_to_irr[:, None] == irr_ids[None, :], home_slot[None, :], 0), axis=1
    )
    member = (stored // per_owner) == me
    q_count = q_to_irr.shape[0]
    q_ids = jnp.arange(q_count, dtype=i32)
    local_q = per_owner * NSYM
    rank = jnp.sum((member[None, :] & (q_ids[None, :] < q_ids[:, None])).astype(i32), axis=1)
    t_ids = jnp.arange(local_q, dtype=i32)
    at_t = member[None, :] & (rank[None, :] == t_ids[:, None])
    q_of = jnp.sum(jnp.where(at_t, q_ids[None, :], 0), axis=1)
    block_of = jnp.sum(jnp.where(at_t, stored[None, :] % per_owner, 0), axis=1)

    pairs = q_all.reshape(-1)
    pair_count = pairs.shape[0]
    run = 128
    same = (pairs.reshape(1, -1, run) == q_of[:, None, None])
    before = (jnp.arange(run)[:, None] < jnp.arange(run)[None, :]).astype(jnp.bfloat16)
    within = lax.dot_general(
        same.astype(jnp.bfloat16).reshape(-1, run), before, (((1,), (0,)), ((), ())),
        preferred_element_type=jnp.float32,
    ).astype(i32).reshape(same.shape)
    per_run = jnp.sum(same.astype(i32), axis=2)
    runs = per_run.shape[1]
    run_ids = jnp.arange(runs, dtype=i32)
    run_start = jnp.sum(
        jnp.where(run_ids[None, :, None] > run_ids[None, None, :], per_run[:, None, :], 0), axis=2
    )
    count = jnp.sum(per_run, axis=1)
    chunks = (count + CHUNK - 1) // CHUNK
    first = jnp.sum(jnp.where(t_ids[:, None] > t_ids[None, :], chunks[None, :], 0), axis=1)
    place = (first * CHUNK)[:, None, None] + run_start[:, :, None] + within
    position = jnp.sum(jnp.where(same, place + 1, 0), axis=0).reshape(-1) - 1
    slots = capacity + local_q * CHUNK
    slot_ids = jnp.arange(slots, dtype=i32)
    pair_ids = jnp.arange(pair_count, dtype=i32)
    filled = jnp.sum(
        jnp.where(position[None, :] == slot_ids[:, None], pair_ids[None, :] + 1, 0), axis=1
    ).reshape(-1, CHUNK)
    table = jnp.where(filled > 0, filled, filled[:, :1]).reshape(-1) - 1
    table = jnp.maximum(table, 0)
    chunk_ids = jnp.arange(slots // CHUNK, dtype=i32)
    of_chunk = (first[:, None] <= chunk_ids[None, :]) & (
        chunk_ids[None, :] < (first + chunks)[:, None]
    )
    chunk_q = jnp.sum(jnp.where(of_chunk, q_of[:, None], 0), axis=0)
    chunk_block = jnp.sum(jnp.where(of_chunk, block_of[:, None], 0), axis=0)
    used = jnp.broadcast_to(jnp.sum(chunks), chunk_q.shape)
    return table, jnp.stack([chunk_q, chunk_block, used])


def owner_kernel(table, meta, val_any, cond_any, w_any, perm_any, out_ref,
                 val_ref, cond_ref, w_ref, perm_ref, moved_0, moved_1, moved_2,
                 carried_0, carried_1, carried_2, sems):
    loads = [
        pltpu.make_async_copy(source, target, sems.at[n])
        for n, (source, target) in enumerate(
            ((perm_any, perm_ref), (val_any, val_ref), (cond_any, cond_ref), (w_any, w_ref))
        )
    ]
    for load in loads:
        load.start()
    half = CHUNK * 16
    g = w_ref.shape[1]
    columns = val_ref.shape[0]
    chunks = meta[2, 0]
    lane_group = lax.broadcasted_iota(jnp.int32, (16, 128), 1) // 16
    out_ref[...] = jnp.zeros_like(out_ref)
    for load in loads:
        load.wait()

    def row_col(pair):
        if columns & (columns - 1) == 0:
            return pair >> (columns.bit_length() - 1), pair & (columns - 1)
        return pair // columns, pair % columns

    def permute(chunk):
        chunk = jnp.minimum(chunk, chunks - 1)
        order = perm_ref[pl.ds(meta[0, chunk], 1), :]
        g_ids = lax.broadcasted_iota(jnp.int32, (g, g), 0)
        shuffle = jnp.where(g_ids == order, 1.0, 0.0).astype(jnp.bfloat16)
        val_rows, cond_rows = [], []
        for p in range(CHUNK):
            row, col = row_col(table[chunk * CHUNK + p])
            val_rows.append(val_ref[col])
            cond_rows.append(cond_ref[row])
        rows = jnp.concatenate(val_rows + cond_rows, axis=0)
        return jnp.dot(rows, shuffle, preferred_element_type=jnp.float32).astype(jnp.bfloat16)

    def carry_over(chunk, val_rows):
        chunk = jnp.minimum(chunk, chunks - 1)
        return lax.dot_general(
            val_rows, w_ref[meta[1, chunk]], (((1,), (1,)), ((), ())),
            preferred_element_type=jnp.float32,
        ).astype(jnp.bfloat16)

    def multiply(chunk, cond_rows, carried):
        chunk = jnp.minimum(chunk, chunks - 1)
        products = -lax.dot_general(
            cond_rows, carried, (((1,), (1,)), ((), ())), preferred_element_type=jnp.float32
        )
        for p in range(CHUNK):
            row, col = row_col(table[chunk * CHUNK + p])
            group = col & 7
            turned = pltpu.roll(
                products[p * 16:(p + 1) * 16, :], ((group - p + 8) & 7) * 16, 1
            ).astype(jnp.bfloat16)
            at = pl.ds(pl.multiple_of((col >> 3) * 128, 128), 128)
            out_ref[row, :, at] = jnp.where(lane_group == group, turned, out_ref[row, :, at])

    moved = (moved_0, moved_1, moved_2)
    carried = (carried_0, carried_1, carried_2)

    @pl.when(chunks > 0)
    def _():
        moved_0[...] = permute(0)
        moved_1[...] = permute(1)
        carried_0[...] = carry_over(0, moved_0[:half, :])

        def three_chunks(i, state):
            for u in range(3):
                chunk, v, w = 3 * i + u, (u + 1) % 3, (u + 2) % 3
                multiply(chunk, moved[u][half:, :], carried[u][...])
                carried[v][...] = carry_over(chunk + 1, moved[v][:half, :])
                moved[w][...] = permute(chunk + 2)
            return state

        lax.fori_loop(0, (chunks + 2) // 3, three_chunks, 0)


def owner_products(table, meta, val_t, cond_t, w_store, g_perm):
    rows, band_pairs, g = cond_t.shape
    columns = val_t.shape[0]
    vmem = pl.BlockSpec(memory_space=pltpu.VMEM)
    anywhere = pl.BlockSpec(memory_space=pl.ANY)
    smem = pl.BlockSpec(memory_space=pltpu.SMEM)
    return pl.pallas_call(
        owner_kernel,
        out_shape=jax.ShapeDtypeStruct((rows, band_pairs, columns * band_pairs), jnp.bfloat16),
        in_specs=[smem, smem, anywhere, anywhere, anywhere, anywhere],
        out_specs=vmem,
        scratch_shapes=[
            *[pltpu.VMEM(x.shape, x.dtype) for x in (val_t, cond_t, w_store, g_perm)],
            *[pltpu.VMEM((2 * CHUNK * band_pairs, g), jnp.bfloat16)] * 3,
            *[pltpu.VMEM((CHUNK * band_pairs, g), jnp.bfloat16)] * 3,
            pltpu.SemaphoreType.DMA((4,)),
        ],
        compiler_params=pltpu.CompilerParams(vmem_limit_bytes=48 * 1024 * 1024),
        cost_estimate=pl.CostEstimate(
            flops=10_000_000_000, bytes_accessed=8_000_000, transcendentals=0
        ),
    )(table, meta, val_t, cond_t, w_store, g_perm)


def gather_kernel(owners, peers, q_ref, cond_ref, val_ref, q_out, cond_out, val_out,
                  send, recv, near_send, near_recv, pass_send, pass_recv, own_sem):
    a, p = lax.axis_index("ka"), lax.axis_index("kp")
    chips = owners // 2
    chip, core = a // 2, lax.rem(a, 2)
    near = a + 1 - 2 * core
    ahead, behind = lax.rem(p + 1, peers), lax.rem(p + peers - 1, peers)
    half = val_ref.shape[0] // 2
    barrier = pltpu.get_barrier_semaphore()
    for step in range(1, chips):
        pl.semaphore_signal(
            barrier, inc=1, device_id=(lax.rem(chip + step, chips) * 2 + core, p),
            device_id_type=MESH,
        )
    for place in ((near, p), (a, ahead), (a, behind)):
        pl.semaphore_signal(barrier, inc=1, device_id=place, device_id_type=MESH)
    pl.semaphore_wait(barrier, chips + 2)

    def started(source, target, sems, place):
        copy = pltpu.make_async_remote_copy(
            src_ref=source, dst_ref=target, send_sem=sems[0], recv_sem=sems[1],
            device_id=place, device_id_type=MESH,
        )
        copy.start()
        return copy

    arrays = ((q_ref, q_out), (cond_ref, cond_out))
    far, done = [], []
    for kind, (source, target) in enumerate(arrays):
        if kind == 1:
            part = pl.ds(core * half, half)
            landing = pl.ds(2 * half + core * half, half)
            last = 2 * (chips - 1)
            panel = started(
                val_ref.at[part], val_out.at[landing], (send.at[last], recv.at[last]), (a, ahead)
            )
        for step in range(1, chips):
            at = kind * (chips - 1) + step - 1
            place = (lax.rem(chip + step, chips) * 2 + core, p)
            far.append(started(source, target.at[a], (send.at[at], recv.at[at]), place))
        done.append(
            started(source, target.at[a], (near_send.at[kind], near_recv.at[kind]), (near, p))
        )
    own = [
        pltpu.make_async_copy(q_ref, q_out.at[a], own_sem.at[0]),
        pltpu.make_async_copy(cond_ref, cond_out.at[a], own_sem.at[1]),
        pltpu.make_async_copy(val_ref, val_out.at[pl.ds(0, 2 * half)], own_sem.at[2]),
    ]
    for copy in own:
        copy.start()
    for kind, (source, target) in enumerate(arrays):
        for step in range(1, chips):
            at = kind * (chips - 1) + step - 1
            far[at].wait_recv()
            origin = lax.rem(chip + chips - step, chips) * 2 + core
            done.append(
                started(
                    target.at[origin], target.at[origin],
                    (pass_send.at[at], pass_recv.at[at]), (near, p),
                )
            )
    panel.wait_recv()
    done.append(
        started(
            val_out.at[landing], val_out.at[landing],
            (pass_send.at[last], pass_recv.at[last]), (near, p),
        )
    )
    for copy in own:
        copy.wait()
    for copy in far + [panel]:
        copy.wait_send()
    for copy in done:
        copy.wait()


def gathered(owners, peers, q_table, cond_t, val_t):
    anywhere = pl.BlockSpec(memory_space=pl.ANY)
    dma = pltpu.SemaphoreType.DMA
    count = owners - 1
    return pl.pallas_call(
        functools.partial(gather_kernel, owners, peers),
        out_shape=(
            jax.ShapeDtypeStruct((owners, *q_table.shape), q_table.dtype),
            jax.ShapeDtypeStruct((owners, *cond_t.shape), cond_t.dtype),
            jax.ShapeDtypeStruct((2 * val_t.shape[0], *val_t.shape[1:]), val_t.dtype),
        ),
        in_specs=[anywhere] * 3,
        out_specs=(anywhere,) * 3,
        scratch_shapes=[
            dma((count,)), dma((count,)), dma((2,)), dma((2,)), dma((count,)), dma((count,)),
            dma((3,)),
        ],
        compiler_params=pltpu.CompilerParams(collective_id=0, has_side_effects=True),
    )(q_table, cond_t, val_t)


def return_kernel(owners, parts_ref, out_ref, landed, send, recv, own_sem):
    a, p = lax.axis_index("ka"), lax.axis_index("kp")
    barrier = pltpu.get_barrier_semaphore()
    for step in range(1, owners):
        pl.semaphore_signal(
            barrier, inc=1, device_id=(lax.rem(a + step, owners), p), device_id_type=MESH
        )
    pl.semaphore_wait(barrier, owners - 1)
    copies = []
    for step in range(1, owners):
        peer = lax.rem(a + step, owners)
        copy = pltpu.make_async_remote_copy(
            src_ref=parts_ref.at[peer], dst_ref=landed.at[step],
            send_sem=send.at[step - 1], recv_sem=recv.at[step - 1],
            device_id=(peer, p), device_id_type=MESH,
        )
        copy.start()
        copies.append(copy)
    own = pltpu.make_async_copy(parts_ref.at[a], landed.at[0], own_sem)
    own.start()
    own.wait()
    out_ref[...] = landed[0].astype(jnp.float32)
    for step in range(1, owners):
        copies[step - 1].wait()
        out_ref[...] += landed[step].astype(jnp.float32)


def returned(owners, parts):
    dma = pltpu.SemaphoreType.DMA
    return pl.pallas_call(
        functools.partial(return_kernel, owners),
        out_shape=jax.ShapeDtypeStruct(parts.shape[1:], jnp.float32),
        in_specs=[pl.BlockSpec(memory_space=pl.ANY)],
        out_specs=pl.BlockSpec(memory_space=pltpu.VMEM),
        scratch_shapes=[
            pltpu.VMEM(parts.shape, parts.dtype), dma((owners - 1,)), dma((owners - 1,)), dma,
        ],
        compiler_params=pltpu.CompilerParams(
            collective_id=1, has_side_effects=True, vmem_limit_bytes=32 * 1024 * 1024
        ),
    )(parts)


def per_device(cond_pairs, val_pairs, w_store, q_table, q_to_irr, g_perm, home_slot):
    owners = lax.axis_size("ka")
    peers = lax.axis_size("kp")
    per_owner = w_store.shape[0]
    row_count = cond_pairs.shape[0]
    band_pairs = cond_pairs.shape[2]
    q_all, cond_t, val_t = gathered(
        owners, peers, q_table, cond_pairs.transpose(0, 2, 1), val_pairs.transpose(0, 2, 1)
    )
    cond_t = cond_t.reshape(owners * row_count, band_pairs, -1)
    capacity = owners * 2 * (3 * row_count * row_count // 2)
    table, meta = pair_lists(q_all, q_to_irr, home_slot, per_owner, capacity)
    parts = owner_products(table, meta, val_t, cond_t, w_store, g_perm)
    columns = val_t.shape[0] * band_pairs
    parts = parts.reshape(owners, row_count * band_pairs, columns)
    return returned(owners, parts)


def solution(mesh):
    placed = (
        P(("ka", "kp"), None, None),
        P("kp", None, None),
        P("ka", None, None),
        P(("ka", "kp"), None),
        P(),
        P(),
        P(),
    )
    return jax.shard_map(
        per_device, mesh=mesh, in_specs=placed, out_specs=P(("ka", "kp"), None), check_vma=False
    )
```

```python
import functools

import jax
import jax.numpy as jnp
from jax import lax
from jax.experimental import pallas as pl
from jax.experimental.pallas import tpu as pltpu
from jax.sharding import PartitionSpec as P

NSYM = 4
CHUNK = 8
MESH = pl.DeviceIdType.MESH


def pair_lists(q_all, q_to_irr, home_slot, per_owner, capacity):
    me = lax.axis_index("ka")
    i32 = jnp.int32
    irr_ids = jnp.arange(home_slot.shape[0], dtype=i32)
    stored = jnp.sum(
        jnp.where(q_to_irr[:, None] == irr_ids[None, :], home_slot[None, :], 0), axis=1
    )
    member = (stored // per_owner) == me
    q_count = q_to_irr.shape[0]
    q_ids = jnp.arange(q_count, dtype=i32)
    local_q = per_owner * NSYM
    rank = jnp.sum((member[None, :] & (q_ids[None, :] < q_ids[:, None])).astype(i32), axis=1)
    t_ids = jnp.arange(local_q, dtype=i32)
    at_t = member[None, :] & (rank[None, :] == t_ids[:, None])
    q_of = jnp.sum(jnp.where(at_t, q_ids[None, :], 0), axis=1)
    block_of = jnp.sum(jnp.where(at_t, stored[None, :] % per_owner, 0), axis=1)

    pairs = q_all.reshape(-1)
    pair_count = pairs.shape[0]
    run = 128
    same = (pairs.reshape(1, -1, run) == q_of[:, None, None])
    before = (jnp.arange(run)[:, None] < jnp.arange(run)[None, :]).astype(jnp.bfloat16)
    within = lax.dot_general(
        same.astype(jnp.bfloat16).reshape(-1, run), before, (((1,), (0,)), ((), ())),
        preferred_element_type=jnp.float32,
    ).astype(i32).reshape(same.shape)
    per_run = jnp.sum(same.astype(i32), axis=2)
    runs = per_run.shape[1]
    run_ids = jnp.arange(runs, dtype=i32)
    run_start = jnp.sum(
        jnp.where(run_ids[None, :, None] > run_ids[None, None, :], per_run[:, None, :], 0), axis=2
    )
    count = jnp.sum(per_run, axis=1)
    chunks = (count + CHUNK - 1) // CHUNK
    first = jnp.sum(jnp.where(t_ids[:, None] > t_ids[None, :], chunks[None, :], 0), axis=1)
    place = (first * CHUNK)[:, None, None] + run_start[:, :, None] + within
    position = jnp.sum(jnp.where(same, place + 1, 0), axis=0).reshape(-1) - 1
    slots = capacity + local_q * CHUNK
    slot_ids = jnp.arange(slots, dtype=i32)
    pair_ids = jnp.arange(pair_count, dtype=i32)
    filled = jnp.sum(
        jnp.where(position[None, :] == slot_ids[:, None], pair_ids[None, :] + 1, 0), axis=1
    ).reshape(-1, CHUNK)
    table = jnp.where(filled > 0, filled, filled[:, :1]).reshape(-1) - 1
    table = jnp.maximum(table, 0)
    chunk_ids = jnp.arange(slots // CHUNK, dtype=i32)
    of_chunk = (first[:, None] <= chunk_ids[None, :]) & (
        chunk_ids[None, :] < (first + chunks)[:, None]
    )
    chunk_q = jnp.sum(jnp.where(of_chunk, q_of[:, None], 0), axis=0)
    chunk_block = jnp.sum(jnp.where(of_chunk, block_of[:, None], 0), axis=0)
    used = jnp.broadcast_to(jnp.sum(chunks), chunk_q.shape)
    return table, jnp.stack([chunk_q, chunk_block, used])


def owner_kernel(table, meta, val_any, next_any, cond_any, w_any, perm_any, out_ref,
                 val_ref, cond_ref, w_ref, perm_ref, moved_0, moved_1, moved_2,
                 carried_0, carried_1, carried_2, sems):
    width = val_any.shape[0]
    loads = [
        pltpu.make_async_copy(source, target, sems.at[n])
        for n, (source, target) in enumerate(
            (
                (perm_any, perm_ref), (val_any, val_ref.at[pl.ds(0, width)]),
                (next_any, val_ref.at[pl.ds(width, width)]), (cond_any, cond_ref), (w_any, w_ref),
            )
        )
    ]
    for load in loads:
        load.start()
    half = CHUNK * 16
    g = w_ref.shape[1]
    columns = val_ref.shape[0]
    chunks = meta[2, 0]
    lane_group = lax.broadcasted_iota(jnp.int32, (16, 128), 1) // 16
    out_ref[...] = jnp.zeros_like(out_ref)
    for load in loads:
        load.wait()

    def row_col(pair):
        if columns & (columns - 1) == 0:
            return pair >> (columns.bit_length() - 1), pair & (columns - 1)
        return pair // columns, pair % columns

    def permute(chunk):
        chunk = jnp.minimum(chunk, chunks - 1)
        order = perm_ref[pl.ds(meta[0, chunk], 1), :]
        g_ids = lax.broadcasted_iota(jnp.int32, (g, g), 0)
        shuffle = jnp.where(g_ids == order, 1.0, 0.0).astype(jnp.bfloat16)
        val_rows, cond_rows = [], []
        for p in range(CHUNK):
            row, col = row_col(table[chunk * CHUNK + p])
            val_rows.append(val_ref[col])
            cond_rows.append(cond_ref[row])
        rows = jnp.concatenate(val_rows + cond_rows, axis=0)
        return jnp.dot(rows, shuffle, preferred_element_type=jnp.float32).astype(jnp.bfloat16)

    def carry_over(chunk, val_rows):
        chunk = jnp.minimum(chunk, chunks - 1)
        return lax.dot_general(
            val_rows, w_ref[meta[1, chunk]], (((1,), (1,)), ((), ())),
            preferred_element_type=jnp.float32,
        ).astype(jnp.bfloat16)

    def multiply(chunk, cond_rows, carried):
        chunk = jnp.minimum(chunk, chunks - 1)
        products = -lax.dot_general(
            cond_rows, carried, (((1,), (1,)), ((), ())), preferred_element_type=jnp.float32
        )
        for p in range(CHUNK):
            row, col = row_col(table[chunk * CHUNK + p])
            group = col & 7
            turned = pltpu.roll(
                products[p * 16:(p + 1) * 16, :], ((group - p + 8) & 7) * 16, 1
            ).astype(jnp.bfloat16)
            at = pl.ds(pl.multiple_of((col >> 3) * 128, 128), 128)
            out_ref[row, :, at] = jnp.where(lane_group == group, turned, out_ref[row, :, at])

    moved = (moved_0, moved_1, moved_2)
    carried = (carried_0, carried_1, carried_2)

    @pl.when(chunks > 0)
    def _():
        moved_0[...] = permute(0)
        moved_1[...] = permute(1)
        carried_0[...] = carry_over(0, moved_0[:half, :])

        def three_chunks(i, state):
            for u in range(3):
                chunk, v, w = 3 * i + u, (u + 1) % 3, (u + 2) % 3
                multiply(chunk, moved[u][half:, :], carried[u][...])
                carried[v][...] = carry_over(chunk + 1, moved[v][:half, :])
                moved[w][...] = permute(chunk + 2)
            return state

        lax.fori_loop(0, (chunks + 2) // 3, three_chunks, 0)


def owner_products(table, meta, val_t, next_t, cond_t, w_store, g_perm):
    rows, band_pairs, g = cond_t.shape
    columns = 2 * val_t.shape[0]
    vmem = pl.BlockSpec(memory_space=pltpu.VMEM)
    anywhere = pl.BlockSpec(memory_space=pl.ANY)
    smem = pl.BlockSpec(memory_space=pltpu.SMEM)
    return pl.pallas_call(
        owner_kernel,
        out_shape=jax.ShapeDtypeStruct((rows, band_pairs, columns * band_pairs), jnp.bfloat16),
        in_specs=[smem, smem, anywhere, anywhere, anywhere, anywhere, anywhere],
        out_specs=vmem,
        scratch_shapes=[
            pltpu.VMEM((columns, band_pairs, g), val_t.dtype),
            *[pltpu.VMEM(x.shape, x.dtype) for x in (cond_t, w_store, g_perm)],
            *[pltpu.VMEM((2 * CHUNK * band_pairs, g), jnp.bfloat16)] * 3,
            *[pltpu.VMEM((CHUNK * band_pairs, g), jnp.bfloat16)] * 3,
            pltpu.SemaphoreType.DMA((5,)),
        ],
        compiler_params=pltpu.CompilerParams(vmem_limit_bytes=62 * 1024 * 1024),
        cost_estimate=pl.CostEstimate(
            flops=10_000_000_000, bytes_accessed=8_000_000, transcendentals=0
        ),
    )(table, meta, val_t, next_t, cond_t, w_store, g_perm)


def gather_kernel(owners, peers, q_ref, cond_ref, val_ref, q_out, cond_out, val_out,
                  send, recv, near_send, near_recv, pass_send, pass_recv, own_sem):
    a, p = lax.axis_index("ka"), lax.axis_index("kp")
    chips = owners // 2
    chip, core = a // 2, lax.rem(a, 2)
    near = a + 1 - 2 * core
    ahead, behind = lax.rem(p + 1, peers), lax.rem(p + peers - 1, peers)
    half = val_ref.shape[0] // 2
    barrier = pltpu.get_barrier_semaphore()
    for step in range(1, chips):
        pl.semaphore_signal(
            barrier, inc=1, device_id=(lax.rem(chip + step, chips) * 2 + core, p),
            device_id_type=MESH,
        )
    for place in ((near, p), (a, ahead), (a, behind)):
        pl.semaphore_signal(barrier, inc=1, device_id=place, device_id_type=MESH)
    pl.semaphore_wait(barrier, chips + 2)

    def started(source, target, sems, place):
        copy = pltpu.make_async_remote_copy(
            src_ref=source, dst_ref=target, send_sem=sems[0], recv_sem=sems[1],
            device_id=place, device_id_type=MESH,
        )
        copy.start()
        return copy

    arrays = ((q_ref, q_out), (cond_ref, cond_out))
    far, done = [], []
    for kind, (source, target) in enumerate(arrays):
        if kind == 1:
            part = pl.ds(core * half, half)
            landing = part
            last = 2 * (chips - 1)
            panel = started(
                val_ref.at[part], val_out.at[landing], (send.at[last], recv.at[last]), (a, ahead)
            )
        for step in range(1, chips):
            at = kind * (chips - 1) + step - 1
            place = (lax.rem(chip + step, chips) * 2 + core, p)
            far.append(started(source, target.at[a], (send.at[at], recv.at[at]), place))
        done.append(
            started(source, target.at[a], (near_send.at[kind], near_recv.at[kind]), (near, p))
        )
    own = [
        pltpu.make_async_copy(q_ref, q_out.at[a], own_sem.at[0]),
        pltpu.make_async_copy(cond_ref, cond_out.at[a], own_sem.at[1]),
    ]
    for copy in own:
        copy.start()
    for kind, (source, target) in enumerate(arrays):
        for step in range(1, chips):
            at = kind * (chips - 1) + step - 1
            far[at].wait_recv()
            origin = lax.rem(chip + chips - step, chips) * 2 + core
            done.append(
                started(
                    target.at[origin], target.at[origin],
                    (pass_send.at[at], pass_recv.at[at]), (near, p),
                )
            )
    panel.wait_recv()
    done.append(
        started(
            val_out.at[landing], val_out.at[landing],
            (pass_send.at[last], pass_recv.at[last]), (near, p),
        )
    )
    for copy in own:
        copy.wait()
    for copy in far + [panel]:
        copy.wait_send()
    for copy in done:
        copy.wait()


def gathered(owners, peers, q_table, cond_t, val_t):
    anywhere = pl.BlockSpec(memory_space=pl.ANY)
    dma = pltpu.SemaphoreType.DMA
    count = owners - 1
    return pl.pallas_call(
        functools.partial(gather_kernel, owners, peers),
        out_shape=(
            jax.ShapeDtypeStruct((owners, *q_table.shape), q_table.dtype),
            jax.ShapeDtypeStruct((owners, *cond_t.shape), cond_t.dtype),
            jax.ShapeDtypeStruct(val_t.shape, val_t.dtype),
        ),
        in_specs=[anywhere] * 3,
        out_specs=(anywhere,) * 3,
        scratch_shapes=[
            dma((count,)), dma((count,)), dma((2,)), dma((2,)), dma((count,)), dma((count,)),
            dma((2,)),
        ],
        compiler_params=pltpu.CompilerParams(collective_id=0, has_side_effects=True),
    )(q_table, cond_t, val_t)


def return_kernel(owners, parts_ref, out_ref, landed, send, recv, own_sem):
    a, p = lax.axis_index("ka"), lax.axis_index("kp")
    barrier = pltpu.get_barrier_semaphore()
    for step in range(1, owners):
        pl.semaphore_signal(
            barrier, inc=1, device_id=(lax.rem(a + step, owners), p), device_id_type=MESH
        )
    pl.semaphore_wait(barrier, owners - 1)
    copies = []
    for step in range(1, owners):
        peer = lax.rem(a + step, owners)
        copy = pltpu.make_async_remote_copy(
            src_ref=parts_ref.at[peer], dst_ref=landed.at[step],
            send_sem=send.at[step - 1], recv_sem=recv.at[step - 1],
            device_id=(peer, p), device_id_type=MESH,
        )
        copy.start()
        copies.append(copy)
    own = pltpu.make_async_copy(parts_ref.at[a], landed.at[0], own_sem)
    own.start()
    own.wait()
    out_ref[...] = landed[0].astype(jnp.float32)
    for step in range(1, owners):
        copies[step - 1].wait()
        out_ref[...] += landed[step].astype(jnp.float32)


def returned(owners, parts):
    dma = pltpu.SemaphoreType.DMA
    return pl.pallas_call(
        functools.partial(return_kernel, owners),
        out_shape=jax.ShapeDtypeStruct(parts.shape[1:], jnp.float32),
        in_specs=[pl.BlockSpec(memory_space=pl.ANY)],
        out_specs=pl.BlockSpec(memory_space=pltpu.VMEM),
        scratch_shapes=[
            pltpu.VMEM(parts.shape, parts.dtype), dma((owners - 1,)), dma((owners - 1,)), dma,
        ],
        compiler_params=pltpu.CompilerParams(
            collective_id=1, has_side_effects=True, vmem_limit_bytes=62 * 1024 * 1024
        ),
    )(parts)


def per_device(cond_pairs, val_pairs, w_store, q_table, q_to_irr, g_perm, home_slot):
    owners = lax.axis_size("ka")
    peers = lax.axis_size("kp")
    per_owner = w_store.shape[0]
    row_count = cond_pairs.shape[0]
    band_pairs = cond_pairs.shape[2]
    val_t = val_pairs.transpose(0, 2, 1)
    q_all, cond_t, next_t = gathered(
        owners, peers, q_table, cond_pairs.transpose(0, 2, 1), val_t
    )
    cond_t = cond_t.reshape(owners * row_count, band_pairs, -1)
    capacity = owners * 2 * (3 * row_count * row_count // 2)
    table, meta = pair_lists(q_all, q_to_irr, home_slot, per_owner, capacity)
    parts = owner_products(table, meta, val_t, next_t, cond_t, w_store, g_perm)
    columns = 2 * val_t.shape[0] * band_pairs
    parts = parts.reshape(owners, row_count * band_pairs, columns)
    return returned(owners, parts)


def solution(mesh):
    placed = (
        P(("ka", "kp"), None, None),
        P("kp", None, None),
        P("ka", None, None),
        P(("ka", "kp"), None),
        P(),
        P(),
        P(),
    )
    return jax.shard_map(
        per_device, mesh=mesh, in_specs=placed, out_specs=P(("ka", "kp"), None), check_vma=False
    )
```

```python
import functools

import jax
import jax.numpy as jnp
from jax import lax
from jax.experimental import pallas as pl
from jax.experimental.pallas import tpu as pltpu
from jax.sharding import PartitionSpec as P

NSYM = 4
CHUNK = 8
MESH = pl.DeviceIdType.MESH


def pair_lists(q_all, q_to_irr, home_slot, per_owner, capacity):
    me = lax.axis_index("ka")
    i32 = jnp.int32
    irr_ids = jnp.arange(home_slot.shape[0], dtype=i32)
    stored = jnp.sum(
        jnp.where(q_to_irr[:, None] == irr_ids[None, :], home_slot[None, :], 0), axis=1
    )
    member = (stored // per_owner) == me
    q_count = q_to_irr.shape[0]
    q_ids = jnp.arange(q_count, dtype=i32)
    local_q = per_owner * NSYM
    rank = jnp.sum((member[None, :] & (q_ids[None, :] < q_ids[:, None])).astype(i32), axis=1)
    t_ids = jnp.arange(local_q, dtype=i32)
    at_t = member[None, :] & (rank[None, :] == t_ids[:, None])
    q_of = jnp.sum(jnp.where(at_t, q_ids[None, :], 0), axis=1)
    block_of = jnp.sum(jnp.where(at_t, stored[None, :] % per_owner, 0), axis=1)

    pairs = q_all.reshape(-1)
    pair_count = pairs.shape[0]
    run = 128
    same = (pairs.reshape(1, -1, run) == q_of[:, None, None])
    before = (jnp.arange(run)[:, None] < jnp.arange(run)[None, :]).astype(jnp.bfloat16)
    within = lax.dot_general(
        same.astype(jnp.bfloat16).reshape(-1, run), before, (((1,), (0,)), ((), ())),
        preferred_element_type=jnp.float32,
    ).astype(i32).reshape(same.shape)
    per_run = jnp.sum(same.astype(i32), axis=2)
    runs = per_run.shape[1]
    run_ids = jnp.arange(runs, dtype=i32)
    run_start = jnp.sum(
        jnp.where(run_ids[None, :, None] > run_ids[None, None, :], per_run[:, None, :], 0), axis=2
    )
    count = jnp.sum(per_run, axis=1)
    chunks = (count + CHUNK - 1) // CHUNK
    first = jnp.sum(jnp.where(t_ids[:, None] > t_ids[None, :], chunks[None, :], 0), axis=1)
    place = (first * CHUNK)[:, None, None] + run_start[:, :, None] + within
    position = jnp.sum(jnp.where(same, place + 1, 0), axis=0).reshape(-1) - 1
    slots = capacity + local_q * CHUNK
    slot_ids = jnp.arange(slots, dtype=i32)
    pair_ids = jnp.arange(pair_count, dtype=i32)
    filled = jnp.sum(
        jnp.where(position[None, :] == slot_ids[:, None], pair_ids[None, :] + 1, 0), axis=1
    ).reshape(-1, CHUNK)
    table = jnp.where(filled > 0, filled, filled[:, :1]).reshape(-1) - 1
    table = jnp.maximum(table, 0)
    chunk_ids = jnp.arange(slots // CHUNK, dtype=i32)
    of_chunk = (first[:, None] <= chunk_ids[None, :]) & (
        chunk_ids[None, :] < (first + chunks)[:, None]
    )
    chunk_q = jnp.sum(jnp.where(of_chunk, q_of[:, None], 0), axis=0)
    chunk_block = jnp.sum(jnp.where(of_chunk, block_of[:, None], 0), axis=0)
    used = jnp.broadcast_to(jnp.sum(chunks), chunk_q.shape)
    return table, jnp.stack([chunk_q, chunk_block, used])


def owner_kernel(table, meta, val_any, next_any, cond_any, w_any, perm_any, out_ref,
                 val_ref, cond_ref, w_ref, perm_ref, moved_0, moved_1, moved_2,
                 carried_0, carried_1, carried_2, sems):
    width = val_any.shape[0]
    loads = [
        pltpu.make_async_copy(source, target, sems.at[n])
        for n, (source, target) in enumerate(
            (
                (perm_any, perm_ref), (val_any, val_ref.at[pl.ds(0, width)]),
                (next_any, val_ref.at[pl.ds(width, width)]), (cond_any, cond_ref), (w_any, w_ref),
            )
        )
    ]
    for load in loads:
        load.start()
    half = CHUNK * 16
    g = w_ref.shape[1]
    columns = val_ref.shape[0]
    chunks = meta[2, 0]
    lane_group = lax.broadcasted_iota(jnp.int32, (16, 128), 1) // 16
    out_ref[...] = jnp.zeros_like(out_ref)
    for load in loads:
        load.wait()

    def row_col(pair):
        if columns & (columns - 1) == 0:
            return pair >> (columns.bit_length() - 1), pair & (columns - 1)
        return pair // columns, pair % columns

    def permute(chunk):
        chunk = jnp.minimum(chunk, chunks - 1)
        order = perm_ref[pl.ds(meta[0, chunk], 1), :]
        g_ids = lax.broadcasted_iota(jnp.int32, (g, g), 0)
        shuffle = jnp.where(g_ids == order, 1.0, 0.0).astype(jnp.bfloat16)
        val_rows, cond_rows = [], []
        for p in range(CHUNK):
            row, col = row_col(table[chunk * CHUNK + p])
            val_rows.append(val_ref[col])
            cond_rows.append(cond_ref[row])
        rows = jnp.concatenate(val_rows + cond_rows, axis=0)
        return jnp.dot(rows, shuffle, preferred_element_type=jnp.float32).astype(jnp.bfloat16)

    def carry_over(chunk, val_rows):
        chunk = jnp.minimum(chunk, chunks - 1)
        return lax.dot_general(
            val_rows, w_ref[meta[1, chunk]], (((1,), (1,)), ((), ())),
            preferred_element_type=jnp.float32,
        ).astype(jnp.bfloat16)

    def multiply(chunk, cond_rows, carried):
        chunk = jnp.minimum(chunk, chunks - 1)
        products = -lax.dot_general(
            cond_rows, carried, (((1,), (1,)), ((), ())), preferred_element_type=jnp.float32
        )
        for p in range(CHUNK):
            row, col = row_col(table[chunk * CHUNK + p])
            group = col & 7
            turned = pltpu.roll(
                products[p * 16:(p + 1) * 16, :], ((group - p + 8) & 7) * 16, 1
            ).astype(jnp.bfloat16)
            at = pl.ds(pl.multiple_of((col >> 3) * 128, 128), 128)
            out_ref[row, :, at] = jnp.where(lane_group == group, turned, out_ref[row, :, at])

    moved = (moved_0, moved_1, moved_2)
    carried = (carried_0, carried_1, carried_2)

    @pl.when(chunks > 0)
    def _():
        moved_0[...] = permute(0)
        moved_1[...] = permute(1)
        carried_0[...] = carry_over(0, moved_0[:half, :])

        def three_chunks(i, state):
            for u in range(3):
                chunk, v, w = 3 * i + u, (u + 1) % 3, (u + 2) % 3
                multiply(chunk, moved[u][half:, :], carried[u][...])
                carried[v][...] = carry_over(chunk + 1, moved[v][:half, :])
                moved[w][...] = permute(chunk + 2)
            return state

        lax.fori_loop(0, (chunks + 2) // 3, three_chunks, 0)


def owner_products(table, meta, val_t, next_t, cond_t, w_store, g_perm):
    rows, band_pairs, g = cond_t.shape
    columns = 2 * val_t.shape[0]
    vmem = pl.BlockSpec(memory_space=pltpu.VMEM)
    anywhere = pl.BlockSpec(memory_space=pl.ANY)
    smem = pl.BlockSpec(memory_space=pltpu.SMEM)
    return pl.pallas_call(
        owner_kernel,
        out_shape=jax.ShapeDtypeStruct((rows, band_pairs, columns * band_pairs), jnp.bfloat16),
        in_specs=[smem, smem, anywhere, anywhere, anywhere, anywhere, anywhere],
        out_specs=vmem,
        scratch_shapes=[
            pltpu.VMEM((columns, band_pairs, g), val_t.dtype),
            *[pltpu.VMEM(x.shape, x.dtype) for x in (cond_t, w_store, g_perm)],
            *[pltpu.VMEM((2 * CHUNK * band_pairs, g), jnp.bfloat16)] * 3,
            *[pltpu.VMEM((CHUNK * band_pairs, g), jnp.bfloat16)] * 3,
            pltpu.SemaphoreType.DMA((5,)),
        ],
        compiler_params=pltpu.CompilerParams(vmem_limit_bytes=62 * 1024 * 1024),
        cost_estimate=pl.CostEstimate(
            flops=10_000_000_000, bytes_accessed=8_000_000, transcendentals=0
        ),
    )(table, meta, val_t, next_t, cond_t, w_store, g_perm)


def gather_kernel(owners, peers, q_ref, cond_ref, val_ref, q_out, cond_out, val_out,
                  send, recv, near_send, near_recv, pass_send, pass_recv, own_sem):
    a, p = lax.axis_index("ka"), lax.axis_index("kp")
    chips = owners // 2
    chip, core = a // 2, lax.rem(a, 2)
    near = a + 1 - 2 * core
    ahead, behind = lax.rem(p + 1, peers), lax.rem(p + peers - 1, peers)
    half = val_ref.shape[0] // 2
    barrier = pltpu.get_barrier_semaphore()
    for step in range(1, chips):
        pl.semaphore_signal(
            barrier, inc=1, device_id=(lax.rem(chip + step, chips) * 2 + core, p),
            device_id_type=MESH,
        )
    for place in ((near, p), (a, ahead), (a, behind)):
        pl.semaphore_signal(barrier, inc=1, device_id=place, device_id_type=MESH)
    pl.semaphore_wait(barrier, chips + 2)

    def started(source, target, sems, place):
        copy = pltpu.make_async_remote_copy(
            src_ref=source, dst_ref=target, send_sem=sems[0], recv_sem=sems[1],
            device_id=place, device_id_type=MESH,
        )
        copy.start()
        return copy

    arrays = ((q_ref, q_out), (cond_ref, cond_out))
    far, done = [], []
    for kind, (source, target) in enumerate(arrays):
        if kind == 1:
            part = pl.ds(core * half, half)
            landing = part
            last = 2 * (chips - 1)
            panel = started(
                val_ref.at[part], val_out.at[landing], (send.at[last], recv.at[last]), (a, ahead)
            )
        for step in range(1, chips):
            at = kind * (chips - 1) + step - 1
            place = (lax.rem(chip + step, chips) * 2 + core, p)
            far.append(started(source, target.at[a], (send.at[at], recv.at[at]), place))
        done.append(
            started(source, target.at[a], (near_send.at[kind], near_recv.at[kind]), (near, p))
        )
    own = [
        pltpu.make_async_copy(q_ref, q_out.at[a], own_sem.at[0]),
        pltpu.make_async_copy(cond_ref, cond_out.at[a], own_sem.at[1]),
    ]
    for copy in own:
        copy.start()
    for kind, (source, target) in enumerate(arrays):
        for step in range(1, chips):
            at = kind * (chips - 1) + step - 1
            far[at].wait_recv()
            origin = lax.rem(chip + chips - step, chips) * 2 + core
            done.append(
                started(
                    target.at[origin], target.at[origin],
                    (pass_send.at[at], pass_recv.at[at]), (near, p),
                )
            )
    panel.wait_recv()
    done.append(
        started(
            val_out.at[landing], val_out.at[landing],
            (pass_send.at[last], pass_recv.at[last]), (near, p),
        )
    )
    for copy in own:
        copy.wait()
    for copy in far + [panel]:
        copy.wait_send()
    for copy in done:
        copy.wait()


def gathered(owners, peers, q_table, cond_t, val_t):
    anywhere = pl.BlockSpec(memory_space=pl.ANY)
    dma = pltpu.SemaphoreType.DMA
    count = owners - 1
    return pl.pallas_call(
        functools.partial(gather_kernel, owners, peers),
        out_shape=(
            jax.ShapeDtypeStruct((owners, *q_table.shape), q_table.dtype),
            jax.ShapeDtypeStruct((owners, *cond_t.shape), cond_t.dtype),
            jax.ShapeDtypeStruct(val_t.shape, val_t.dtype),
        ),
        in_specs=[anywhere] * 3,
        out_specs=(anywhere,) * 3,
        scratch_shapes=[
            dma((count,)), dma((count,)), dma((2,)), dma((2,)), dma((count,)), dma((count,)),
            dma((2,)),
        ],
        compiler_params=pltpu.CompilerParams(collective_id=0, has_side_effects=True),
    )(q_table, cond_t, val_t)


def return_kernel(owners, parts_ref, out_ref, landed, send, recv, own_sem):
    a, p = lax.axis_index("ka"), lax.axis_index("kp")
    barrier = pltpu.get_barrier_semaphore()
    for step in range(1, owners):
        pl.semaphore_signal(
            barrier, inc=1, device_id=(lax.rem(a + step, owners), p), device_id_type=MESH
        )
    pl.semaphore_wait(barrier, owners - 1)
    copies = []
    for step in range(1, owners):
        peer = lax.rem(a + step, owners)
        copy = pltpu.make_async_remote_copy(
            src_ref=parts_ref.at[peer], dst_ref=landed.at[step],
            send_sem=send.at[step - 1], recv_sem=recv.at[step - 1],
            device_id=(peer, p), device_id_type=MESH,
        )
        copy.start()
        copies.append(copy)
    own = pltpu.make_async_copy(parts_ref.at[a], landed.at[0], own_sem)
    own.start()
    own.wait()
    out_ref[...] = landed[0].astype(jnp.float32)
    for step in range(1, owners):
        copies[step - 1].wait()
        out_ref[...] += landed[step].astype(jnp.float32)


def returned(owners, parts):
    dma = pltpu.SemaphoreType.DMA
    return pl.pallas_call(
        functools.partial(return_kernel, owners),
        out_shape=jax.ShapeDtypeStruct(parts.shape[1:], jnp.float32),
        in_specs=[pl.BlockSpec(memory_space=pl.ANY)],
        out_specs=pl.BlockSpec(memory_space=pltpu.VMEM),
        scratch_shapes=[
            pltpu.VMEM(parts.shape, parts.dtype), dma((owners - 1,)), dma((owners - 1,)), dma,
        ],
        compiler_params=pltpu.CompilerParams(
            collective_id=1, has_side_effects=True, vmem_limit_bytes=32 * 1024 * 1024
        ),
    )(parts)


def per_device(cond_pairs, val_pairs, w_store, q_table, q_to_irr, g_perm, home_slot):
    owners = lax.axis_size("ka")
    peers = lax.axis_size("kp")
    per_owner = w_store.shape[0]
    row_count = cond_pairs.shape[0]
    band_pairs = cond_pairs.shape[2]
    val_t = val_pairs.transpose(0, 2, 1)
    q_all, cond_t, next_t = gathered(
        owners, peers, q_table, cond_pairs.transpose(0, 2, 1), val_t
    )
    cond_t = cond_t.reshape(owners * row_count, band_pairs, -1)
    capacity = owners * 2 * (3 * row_count * row_count // 2)
    table, meta = pair_lists(q_all, q_to_irr, home_slot, per_owner, capacity)
    parts = owner_products(table, meta, val_t, next_t, cond_t, w_store, g_perm)
    columns = 2 * val_t.shape[0] * band_pairs
    parts = parts.reshape(owners, row_count * band_pairs, columns)
    return returned(owners, parts)


def solution(mesh):
    placed = (
        P(("ka", "kp"), None, None),
        P("kp", None, None),
        P("ka", None, None),
        P(("ka", "kp"), None),
        P(),
        P(),
        P(),
    )
    return jax.shard_map(
        per_device, mesh=mesh, in_specs=placed, out_specs=P(("ka", "kp"), None), check_vma=False
    )
```
